512 devices in a mesh: dp: 8 (over x, core), expert: 64 (over z, y).
Axes of the slice: x: 4, y: 8, z: 8, core: 2. Of those that a mesh axis runs over, the one named last changes fastest.
Arguments:
- tokens: bfloat16 [65536, 1024], P(('dp', 'expert')), may hold values from -6 to 6
- routes: int32 [65536, 6], P(('dp', 'expert')), may hold values from 0 to 63, all different within a row; in each aligned block of 128 rows (0 to 127, 128 to 255, ...) at most 24 rows name the same one
- route_weights: float32 [65536, 6], P(('dp', 'expert')), may hold values from 0.1 to 1
- gate_weight: bfloat16 [64, 1024, 512], P('expert'), may hold values from -0.1875 to 0.1875
- up_weight: bfloat16 [64, 1024, 512], P('expert'), may hold values from -0.1875 to 0.1875
- down_weight: bfloat16 [64, 512, 1024], P('expert'), may hold values from -0.25 to 0.25
- cotangent: bfloat16 [65536, 1024], P(('dp', 'expert')), may hold values from -3 to 3
Outputs:
- mixed_latent: bfloat16 [65536, 1024], P(('dp', 'expert'))
- latent_grad: bfloat16 [65536, 1024], P(('dp', 'expert'))
- gate_grad: float32 [64, 1024, 512], P('expert', 'dp')
- up_grad: float32 [64, 1024, 512], P('expert', 'dp')
- down_grad: float32 [64, 512, 1024], P('expert', None, 'dp')
The draws below stay inside these ranges and needn't reach their ends.
Inputs may be any that keep to these rules, and one draw needn't show every extreme that they name: `routes`: each row names 6 different experts. In each aligned block of 128 rows (the rows of one device) no expert is named by more than 24 rows, and some expert is named by exactly 24 rows in some block.
All inputs are finite; a program needn't handle non-finite values.
Results may differ from the reference program's by a relative error of at most 0.015.
Values may be sent and summed in bfloat16 or wider, within the bound.
No kernel may reach another device: no remote copies, remote signals or barrier semaphores. Data moves between devices by JAX's collectives and lax.ppermute only.
A program may use at most 64 MiB of HBM per device.

```python
import math
import jax
import jax.numpy as jnp
import numpy as np
from jax import lax

LATENT = 1024
FFN = 512
TOP = 6
TOK_DEV = 128
EXPERTS = 64
CAPACITY = 12
TOKENS = 65536
N_DP = 8
N_EXPERT = 64


def level_of(key, extent, shards, low, top_value):
    gain, own = 1.0, jax.random.fold_in(key, 6)
    for axis_at, parts in shards:
        heights = jnp.exp(jax.random.uniform(jax.random.fold_in(own, axis_at), (parts,), jnp.float32, low / len(shards), top_value / len(shards)))
        gain = gain * jnp.repeat(heights, extent[axis_at] // parts).reshape([-1 if axis == axis_at else 1 for axis in range(len(extent))])
    return gain


def routed_block(key, own, number, rows, count, top, reach, skew):
    sequence = jax.random.permutation(key, count)
    crowded, usual = portions_of(count, rows * top, reach, skew, True), portions_of(count, rows * top, reach, skew, False)
    places = jnp.arange(count)

    def named(tallies, turn):
        used = int((tallies > 0).sum())
        fixed = max(1, used // 4)
        shifted = fixed + (places - fixed + turn * (used - fixed)) % max(1, count - fixed)
        return jnp.zeros((count,), jnp.int32).at[sequence[jnp.where(places < fixed, places, shifted)]].set(jnp.asarray(tallies, jnp.int32))

    tallies = jnp.where(number % 4 == 0, named(crowded, number // 4), named(usual, number - number // 4 - 1))
    mixed = jax.random.permutation(jax.random.fold_in(own, 3), count)
    giver, sink = mixed[0:count // 2 * 2:2], mixed[1:count // 2 * 2:2]
    slack = jnp.minimum(tallies[giver] - 1, reach - tallies[sink]) // 2
    slack = jnp.where((giver == sequence[0]) | (sink == sequence[0]) | (tallies[sink] == 0), 0, jnp.maximum(slack, 0))
    shifted = jax.random.randint(jax.random.fold_in(own, 4), (count // 2,), 0, 1 << 20) % (slack + 1)
    tallies = tallies.at[giver].add(-shifted).at[sink].add(shifted)
    items = jnp.searchsorted(jnp.cumsum(tallies), jnp.arange(rows * top), side="right").astype(jnp.int32)
    grid = items.reshape(top, rows).T
    grid = grid[jax.random.permutation(jax.random.fold_in(own, 1), rows)]
    turn = jax.random.randint(jax.random.fold_in(own, 2), (rows, 1), 0, top)
    return jnp.take_along_axis(grid, (jnp.arange(top)[None, :] + turn) % top, axis=1)


def portions_of(count, total, most, lean, full):
    loads = [(1 << 20) // math.isqrt(grade ** lean) + 1 for grade in range(1, count + 1)]
    largest = most if full else min(most, max(-(-total // count), total * loads[0] // sum(loads)))
    least = 1 if total - largest >= count - 1 else 0
    given, spare = [largest] + [least] * (count - 1), total - largest - least * (count - 1)
    while spare > 0:
        movable = [i for i in range(1, count) if given[i] < largest] or [i for i in range(1, count) if given[i] < most]
        whole, budget = sum([loads[i] for i in movable]), spare
        for i in movable:
            addition = min(most - given[i], max(1, budget * loads[i] // whole), spare)
            given[i] = given[i] + addition
            spare = spare - addition
    return np.array(given)


def noise(own_key, extent, width, limit, split=(), kind=jnp.bfloat16):
    values = width * jax.random.normal(own_key, extent, jnp.float32)
    if split:
        values = values * level_of(own_key, extent, split, -0.22, 0.18)
    return jnp.clip(values, -limit, limit).astype(kind)


def setup_inputs(seed: int = 0) -> dict:
    seeds = jax.random.split(jax.random.key(seed), 8)
    tokens = noise(seeds[0], (TOKENS, LATENT), 1.0, 6.0, ((0, 512),))
    routes_keys = jax.random.split(jax.random.fold_in(seeds[1], 1), TOKENS // TOK_DEV)
    routes_turns = jax.random.permutation(jax.random.fold_in(seeds[1], 3), TOKENS // TOK_DEV)
    routes = jax.vmap(lambda own, number: routed_block(jax.random.fold_in(seeds[1], 2), own, number, TOK_DEV, EXPERTS, TOP, 2 * CAPACITY, 2))(routes_keys, routes_turns).reshape((TOKENS, TOP))
    route_weights = jnp.clip(jnp.exp(math.log(1.0) - 2.3025851 * jax.random.uniform(seeds[2], (TOKENS, TOP), jnp.float32) ** level_of(seeds[2], (TOKENS, TOP), ((0, 512),), -0.2, 0.2)), 0.1, 1.0)
    gate_weight = noise(seeds[3], (EXPERTS, LATENT, FFN), LATENT ** -0.5, 0.1875, ((0, 64),))
    up_weight = noise(seeds[4], (EXPERTS, LATENT, FFN), LATENT ** -0.5, 0.1875, ((0, 64),))
    down_weight = noise(seeds[5], (EXPERTS, FFN, LATENT), FFN ** -0.5, 0.25, ((0, 64),))
    cotangent = noise(seeds[6], (TOKENS, LATENT), 0.5, 3.0, ((0, 512),))
    return dict(tokens=tokens, routes=routes, route_weights=route_weights, gate_weight=gate_weight, up_weight=up_weight, down_weight=down_weight, cotangent=cotangent)


def slot_plan(route_rows, experts, capacity):
    flat_routes = route_rows.reshape(-1)
    one_hot = (flat_routes[:, None] == jnp.arange(experts, dtype=jnp.int32)[None, :]).astype(jnp.int32)
    earlier = jnp.cumsum(one_hot, axis=0) - one_hot
    slot_rank = jnp.sum(earlier * one_hot, axis=1)
    kept_mask = slot_rank < capacity
    slot_index = jnp.where(kept_mask, flat_routes * capacity + slot_rank, experts * capacity).astype(jnp.int32)
    return kept_mask, slot_index


def pack_rows(row_values, slot_index, experts, capacity):
    latent_width = row_values.shape[1]
    buffer = jnp.zeros((experts * capacity + 1, latent_width), row_values.dtype)
    buffer = buffer.at[slot_index].set(row_values)
    return buffer[:-1].reshape(experts, capacity, latent_width)


def unpack_rows(buffer, slot_index, top_count):
    latent_width = buffer.shape[-1]
    padded = jnp.concatenate([buffer.reshape(-1, latent_width), jnp.zeros((1, latent_width), buffer.dtype)], axis=0)
    return padded[slot_index].reshape(-1, top_count, latent_width)


def expert_forward(inputs, gate_matrix, up_matrix, down_matrix):
    gate_pre = jnp.dot(inputs, gate_matrix, preferred_element_type=jnp.float32)
    up_pre = jnp.dot(inputs, up_matrix, preferred_element_type=jnp.float32)
    hidden = (jax.nn.silu(gate_pre) * up_pre).astype(jnp.bfloat16)
    outputs = jnp.dot(hidden, down_matrix, preferred_element_type=jnp.float32).astype(jnp.bfloat16)
    return outputs, gate_pre, up_pre, hidden


def expert_backward(out_grads, gate_pre, up_pre, gate_matrix, up_matrix, down_matrix):
    contract_last = (((1,), (1,)), ((), ()))
    hidden_grad = lax.dot_general(out_grads, down_matrix, contract_last, preferred_element_type=jnp.float32)
    sigmoid_gate = jax.nn.sigmoid(gate_pre)
    up_grad_pre = (hidden_grad * gate_pre * sigmoid_gate).astype(jnp.bfloat16)
    gate_grad_pre = (hidden_grad * up_pre * sigmoid_gate * (1.0 + gate_pre * (1.0 - sigmoid_gate))).astype(jnp.bfloat16)
    input_grads = lax.dot_general(gate_grad_pre, gate_matrix, contract_last, preferred_element_type=jnp.float32)
    input_grads = input_grads + lax.dot_general(up_grad_pre, up_matrix, contract_last, preferred_element_type=jnp.float32)
    return input_grads.astype(jnp.bfloat16), gate_grad_pre, up_grad_pre


def one_expert(operands):
    inputs, out_grads, gate_matrix, up_matrix, down_matrix = operands
    contract_rows = (((0,), (0,)), ((), ()))
    outputs, gate_pre, up_pre, hidden = expert_forward(inputs, gate_matrix, up_matrix, down_matrix)
    input_grads, gate_grad_pre, up_grad_pre = expert_backward(out_grads, gate_pre, up_pre, gate_matrix, up_matrix, down_matrix)
    gate_part = lax.dot_general(inputs, gate_grad_pre, contract_rows, preferred_element_type=jnp.float32).astype(jnp.bfloat16)
    up_part = lax.dot_general(inputs, up_grad_pre, contract_rows, preferred_element_type=jnp.float32).astype(jnp.bfloat16)
    down_part = lax.dot_general(hidden, out_grads, contract_rows, preferred_element_type=jnp.float32).astype(jnp.bfloat16)
    return outputs, input_grads, gate_part, up_part, down_part


def reference(tokens, routes, route_weights, gate_weight, up_weight, down_weight, cotangent):
    group_arrays = (
        tokens.reshape(N_DP, N_EXPERT, TOK_DEV, LATENT),
        routes.reshape(N_DP, N_EXPERT, TOK_DEV, TOP),
        route_weights.reshape(N_DP, N_EXPERT, TOK_DEV, TOP),
        cotangent.reshape(N_DP, N_EXPERT, TOK_DEV, LATENT),
    )

    def one_group(totals, arrays):
        group_tokens, group_routes, group_weights, group_cotangent = arrays
        kept_mask, slot_index = jax.vmap(lambda route_rows: slot_plan(route_rows, EXPERTS, CAPACITY))(group_routes)
        kept_weights = group_weights * kept_mask.reshape(N_EXPERT, TOK_DEV, TOP).astype(jnp.float32)
        token_rows = jnp.repeat(group_tokens, TOP, axis=1)
        grad_rows = (kept_weights[..., None] * group_cotangent[:, :, None, :].astype(jnp.float32)).astype(jnp.bfloat16)
        grad_rows = grad_rows.reshape(N_EXPERT, TOK_DEV * TOP, LATENT)
        packer = jax.vmap(lambda row_values, positions: pack_rows(row_values, positions, EXPERTS, CAPACITY))
        inbox_tokens = packer(token_rows, slot_index).transpose(1, 0, 2, 3).reshape(EXPERTS, N_EXPERT * CAPACITY, LATENT)
        inbox_grads = packer(grad_rows, slot_index).transpose(1, 0, 2, 3).reshape(EXPERTS, N_EXPERT * CAPACITY, LATENT)
        outputs, input_grads, gate_part, up_part, down_part = lax.map(
            one_expert, (inbox_tokens, inbox_grads, gate_weight, up_weight, down_weight))

        def combine(slot_values):
            per_source = slot_values.reshape(EXPERTS, N_EXPERT, CAPACITY, LATENT).transpose(1, 0, 2, 3)
            gathered = jax.vmap(lambda buffer, positions: unpack_rows(buffer, positions, TOP))(per_source, slot_index)
            return gathered.astype(jnp.float32)

        mixed_latent = jnp.sum(combine(outputs) * kept_weights[..., None], axis=2).astype(jnp.bfloat16)
        latent_grad = jnp.sum(combine(input_grads), axis=2).astype(jnp.bfloat16)
        totals = (totals[0] + gate_part.astype(jnp.float32),
                  totals[1] + up_part.astype(jnp.float32),
                  totals[2] + down_part.astype(jnp.float32))
        return totals, (mixed_latent, latent_grad)

    initial = (jnp.zeros((EXPERTS, LATENT, FFN), jnp.float32),
               jnp.zeros((EXPERTS, LATENT, FFN), jnp.float32),
               jnp.zeros((EXPERTS, FFN, LATENT), jnp.float32))
    totals, (mixed_latent, latent_grad) = lax.scan(one_group, initial, group_arrays)
    return (mixed_latent.reshape(TOKENS, LATENT), latent_grad.reshape(TOKENS, LATENT),
            totals[0], totals[1], totals[2])
```

```python
import jax
import jax.numpy as jnp
from jax import lax
from jax.experimental import pallas as pl
from jax.experimental.pallas import tpu as pltpu
from jax.sharding import PartitionSpec as P

INTERPRET = False
F32 = jnp.float32
BF16 = jnp.bfloat16
NT = (((1,), (1,)), ((), ()))


def chunk_slot(row):
    slot = jnp.where(row < 12, row, jnp.where(row < 16, row - 4, row - 16))
    return slot.astype(F32), row >= 12


def route_tables(routes, weights, experts):
    top_count, token_count = routes.shape
    expert = lax.broadcasted_iota(jnp.int32, (experts, token_count), 0)
    named = jnp.zeros((experts, token_count), F32)
    weight = jnp.zeros((experts, token_count), F32)
    for k in range(top_count):
        same = routes[k : k + 1, :] == expert
        named = jnp.where(same, 1.0, named)
        weight = jnp.where(same, weights[k : k + 1, :], weight)
    earlier = lax.broadcasted_iota(jnp.int32, (token_count, token_count), 0)
    later = lax.broadcasted_iota(jnp.int32, (token_count, token_count), 1)
    before = jnp.where(earlier < later, 1.0, 0.0).astype(BF16)
    rank = jnp.dot(named.astype(BF16), before, preferred_element_type=F32)
    return jnp.where(named > 0.0, rank, -1.0), weight


def pack_kernel(experts, chunk, routes_ref, weights_ref, tokens_ref, cot_ref, send_ref, pick_ref, scale_ref):
    token_count = tokens_ref.shape[0]

    @pl.when(pl.program_id(0) == 0)
    def _():
        rank, weight = route_tables(routes_ref[...], weights_ref[...], experts)
        full = (experts, chunk, token_count)
        row = lax.broadcasted_iota(jnp.int32, full, 1)
        slot, backward = chunk_slot(row)
        hit = jnp.broadcast_to(rank[:, None, :], full) == slot
        one = jnp.where(hit, 1.0, 0.0)
        pick_ref[:, :token_count] = (
            jnp.where(backward, 0.0, one).reshape(experts * chunk, token_count).astype(BF16)
        )
        pick_ref[:, token_count:] = (
            jnp.where(backward, one, 0.0).reshape(experts * chunk, token_count).astype(BF16)
        )
        chosen = jnp.where(hit, jnp.broadcast_to(weight[:, None, :], full), 0.0)
        scale = jnp.where(backward, jnp.sum(chosen, axis=2, keepdims=True), 1.0)
        scale_ref[...] = scale.reshape(experts * chunk, token_count)

    rows = jnp.concatenate([tokens_ref[...], cot_ref[...]], axis=0)
    picked = jnp.dot(pick_ref[...], rows, preferred_element_type=F32)
    width = picked.shape[1]
    scale = scale_ref[...]
    for at in range(0, width, token_count):
        send_ref[:, at : at + token_count] = (picked[:, at : at + token_count] * scale).astype(BF16)


def pack(tokens, cotangent, routes, weights, experts, chunk):
    token_count, width = tokens.shape
    block = 256
    small = pl.BlockSpec(routes.shape, lambda j: (0, 0))
    wide = pl.BlockSpec((token_count, block), lambda j: (0, j))
    rows = experts * chunk
    return pl.pallas_call(
        lambda *refs: pack_kernel(experts, chunk, *refs),
        grid=(width // block,),
        in_specs=[small, small, wide, wide],
        out_specs=pl.BlockSpec((rows, block), lambda j: (0, j)),
        out_shape=jax.ShapeDtypeStruct((rows, width), BF16),
        scratch_shapes=[pltpu.VMEM((rows, 2 * token_count), BF16), pltpu.VMEM((rows, token_count), F32)],
        compiler_params=pltpu.CompilerParams(vmem_limit_bytes=32 * 1024 * 1024),
        cost_estimate=pl.CostEstimate(
            flops=4 * rows * token_count * width, bytes_accessed=2 * (rows + 2 * token_count) * width, transcendentals=0
        ),
        interpret=INTERPRET,
        name="pack",
    )(routes, weights, tokens, cotangent)


def plan_kernel(experts, chunk, routes_ref, weights_ref, plan_ref):
    token_count = routes_ref.shape[1]
    rank, weight = route_tables(routes_ref[...], weights_ref[...], 128)
    rank, weight = rank.T[:, :experts], weight.T[:, :experts]
    rows = experts * chunk
    owner = lax.broadcasted_iota(jnp.int32, (experts, rows), 0) * chunk
    place = lax.broadcasted_iota(jnp.int32, (experts, rows), 1) - owner
    spread = jnp.where((place >= 0) & (place < chunk), 1.0, 0.0).astype(BF16)

    def widen(values):
        return jnp.dot(values.astype(BF16), spread, preferred_element_type=F32)

    coarse = weight.astype(BF16).astype(F32)
    row = lax.rem(lax.broadcasted_iota(jnp.int32, (token_count, rows), 1), chunk)
    slot, backward = chunk_slot(row)
    hit = widen(rank) == slot
    ahead = jnp.where(backward, 0.0, jnp.where(hit, 1.0, 0.0))
    plan_ref[:token_count, :] = (widen(coarse) * ahead).astype(BF16)
    plan_ref[token_count : 2 * token_count, :] = (widen(weight - coarse) * ahead).astype(BF16)
    plan_ref[2 * token_count :, :] = jnp.where(backward & hit, 1.0, 0.0).astype(BF16)


def plan_unpack(routes, weights, experts, chunk):
    token_count = routes.shape[1]
    rows = experts * chunk
    return pl.pallas_call(
        lambda *refs: plan_kernel(experts, chunk, *refs),
        out_shape=jax.ShapeDtypeStruct((3 * token_count, rows), BF16),
        compiler_params=pltpu.CompilerParams(vmem_limit_bytes=32 * 1024 * 1024),
        cost_estimate=pl.CostEstimate(
            flops=6 * token_count * rows * experts, bytes_accessed=6 * token_count * rows, transcendentals=0
        ),
        interpret=INTERPRET,
        name="plan",
    )(routes, weights)


def unpack_kernel(plan_ref, back_ref, share_ref, mixed_ref, grad_ref, gate_ref, up_ref, down_ref):
    token_count = mixed_ref.shape[0]
    total = jnp.dot(plan_ref[...], back_ref[...], preferred_element_type=F32)
    mixed_ref[...] = (total[:token_count] + total[token_count : 2 * token_count]).astype(BF16)
    grad_ref[...] = total[2 * token_count :].astype(BF16)
    gate_ref[0] = share_ref[0].astype(F32)
    up_ref[0] = share_ref[1].astype(F32)
    down_ref[0] = share_ref[2].astype(F32).T


def unpack(plan, back, share):
    token_count = plan.shape[0] // 3
    rows, width = back.shape
    depth = share.shape[0]
    ffn = share.shape[1] // 3
    steps = 4
    block, part = width // steps, ffn // steps
    out = pl.BlockSpec((token_count, block), lambda j: (0, j))
    grad = pl.BlockSpec((1, depth, part), lambda j: (0, 0, j))
    return pl.pallas_call(
        lambda plan_ref, back_ref, gate_in, up_in, down_in, *refs: unpack_kernel(
            plan_ref, back_ref, (gate_in[...], up_in[...], down_in[...]), *refs
        ),
        grid=(steps,),
        in_specs=[
            pl.BlockSpec(plan.shape, lambda j: (0, 0)),
            pl.BlockSpec((rows, block), lambda j: (0, j)),
            pl.BlockSpec((depth, part), lambda j: (0, j)),
            pl.BlockSpec((depth, part), lambda j: (0, steps + j)),
            pl.BlockSpec((depth, part), lambda j: (0, 2 * steps + j)),
        ],
        out_specs=[out, out, grad, grad, pl.BlockSpec((1, part, depth), lambda j: (0, j, 0))],
        out_shape=[
            jax.ShapeDtypeStruct((token_count, width), BF16),
            jax.ShapeDtypeStruct((token_count, width), BF16),
            jax.ShapeDtypeStruct((1, depth, ffn), F32),
            jax.ShapeDtypeStruct((1, depth, ffn), F32),
            jax.ShapeDtypeStruct((1, ffn, depth), F32),
        ],
        compiler_params=pltpu.CompilerParams(vmem_limit_bytes=32 * 1024 * 1024),
        cost_estimate=pl.CostEstimate(
            flops=6 * token_count * rows * width, bytes_accessed=2 * (rows + 5 * token_count) * width, transcendentals=0
        ),
        interpret=INTERPRET,
        name="unpack",
    )(plan, back, share, share, share)


def weight_kernel(inputs_ref, grads_ref, pair_ref, hidden_ref, part_ref):
    contract_rows = (((0,), (0,)), ((), ()))
    both = pair_ref.shape[1]
    pair = lax.dot_general(inputs_ref[...], pair_ref[...], contract_rows, preferred_element_type=F32)
    part_ref[:, :both] = pair.astype(BF16)
    down = lax.dot_general(grads_ref[...], hidden_ref[...], contract_rows, preferred_element_type=F32)
    part_ref[:, both:] = down.astype(BF16)


def weight_parts(inputs, grads, pair_grads, hidden):
    slots, width = inputs.shape
    columns = pair_grads.shape[1] + hidden.shape[1]
    block = 256
    narrow = pl.BlockSpec((slots, block), lambda i: (0, i))
    whole = lambda array: pl.BlockSpec(array.shape, lambda i: (0, 0))
    return pl.pallas_call(
        weight_kernel,
        grid=(width // block,),
        in_specs=[narrow, narrow, whole(pair_grads), whole(hidden)],
        out_specs=pl.BlockSpec((block, columns), lambda i: (i, 0)),
        out_shape=jax.ShapeDtypeStruct((width, columns), BF16),
        compiler_params=pltpu.CompilerParams(vmem_limit_bytes=32 * 1024 * 1024),
        cost_estimate=pl.CostEstimate(
            flops=2 * slots * width * columns, bytes_accessed=2 * (slots + width) * columns, transcendentals=0
        ),
        interpret=INTERPRET,
        name="weight_parts",
    )(inputs, grads, pair_grads, hidden)


def roll_half(values):
    return pltpu.roll(values, 4, 1)


def expert_kernel(sources, inbox_ref, gate_ref, up_ref, down_ref, back_ref, tokens_ref, grads_ref, pair_ref, hidden_ref):
    width = inbox_ref.shape[1]
    ffn = gate_ref.shape[1]
    head = 8 * sources
    piece = 256
    for at in range(0, width, piece):
        cols = slice(at, at + piece)
        got = inbox_ref[:, cols].astype(F32).reshape(sources, 24, piece)
        both = got[:, 8:16].reshape(sources // 2, 2, 8, piece)
        first, second = both[:, 0], both[:, 1]
        low = lax.broadcasted_iota(jnp.int32, first.shape, 1) < 4
        tokens_ref[:head, cols] = got[:, :8].reshape(head, piece).astype(BF16)
        grads_ref[:head, cols] = got[:, 16:].reshape(head, piece).astype(BF16)
        tokens_ref[head:, cols] = jnp.where(low, first, roll_half(second)).reshape(-1, piece).astype(BF16)
        grads_ref[head:, cols] = jnp.where(low, roll_half(first), second).reshape(-1, piece).astype(BF16)
    tokens, grads = tokens_ref[...], grads_ref[...]
    gate_pre = jnp.dot(tokens, gate_ref[...], preferred_element_type=F32)
    up_pre = jnp.dot(tokens, up_ref[...], preferred_element_type=F32)
    hidden_grad = lax.dot_general(grads, down_ref[...], NT, preferred_element_type=F32)
    sigmoid = jax.nn.sigmoid(gate_pre)
    silu = gate_pre * sigmoid
    hidden = (silu * up_pre).astype(BF16)
    up_grad_pre = (hidden_grad * silu).astype(BF16)
    gate_grad_pre = (hidden_grad * up_pre * sigmoid * (1.0 + gate_pre * (1.0 - sigmoid))).astype(BF16)
    hidden_ref[...] = hidden
    pair_ref[:, :ffn] = gate_grad_pre
    pair_ref[:, ffn:] = up_grad_pre
    for at in range(0, width, piece):
        cols = slice(at, at + piece)
        outputs = jnp.dot(hidden, down_ref[:, cols], preferred_element_type=F32)
        slot = lax.dot_general(gate_grad_pre, gate_ref[cols, :], NT, preferred_element_type=F32)
        slot = slot + lax.dot_general(up_grad_pre, up_ref[cols, :], NT, preferred_element_type=F32)
        out_tail = outputs[head:].reshape(sources // 2, 8, piece)
        slot_tail = slot[head:].reshape(sources // 2, 8, piece)
        low = lax.broadcasted_iota(jnp.int32, out_tail.shape, 1) < 4
        first = jnp.where(low, out_tail, roll_half(slot_tail))
        second = jnp.where(low, roll_half(out_tail), slot_tail)
        middle = jnp.concatenate([first[:, None], second[:, None]], axis=1).reshape(sources, 8, piece)
        sent = jnp.concatenate(
            [outputs[:head].reshape(sources, 8, piece), middle, slot[:head].reshape(sources, 8, piece)], axis=1
        )
        back_ref[:, cols] = sent.reshape(24 * sources, piece).astype(BF16)


def run_expert(inbox, gate, up, down, sources, step):
    rows, width = inbox.shape
    ffn = gate.shape[1]
    slots = rows // 2
    part = lambda count, columns: pl.BlockSpec((count, columns), lambda i: (i, 0))
    whole = lambda array: pl.BlockSpec(array.shape, lambda i: (0, 0))
    many, few = 24 * step, 12 * step
    return pl.pallas_call(
        lambda *refs: expert_kernel(step, *refs),
        grid=(sources // step,),
        in_specs=[part(many, width), whole(gate), whole(up), whole(down)],
        out_specs=[part(many, width), part(few, width), part(few, width), part(few, 2 * ffn), part(few, ffn)],
        out_shape=[
            jax.ShapeDtypeStruct((rows, width), BF16),
            jax.ShapeDtypeStruct((slots, width), BF16),
            jax.ShapeDtypeStruct((slots, width), BF16),
            jax.ShapeDtypeStruct((slots, 2 * ffn), BF16),
            jax.ShapeDtypeStruct((slots, ffn), BF16),
        ],
        compiler_params=pltpu.CompilerParams(vmem_limit_bytes=48 * 1024 * 1024),
        cost_estimate=pl.CostEstimate(
            flops=12 * slots * width * ffn, bytes_accessed=14 * slots * width, transcendentals=slots * ffn
        ),
        interpret=INTERPRET,
        name="expert",
    )(inbox, gate, up, down)


def shards(tokens, routes, route_weights, gate_weight, up_weight, down_weight, cotangent):
    token_count, width = tokens.shape
    top_count = routes.shape[1]
    experts = lax.axis_size("expert")
    chunk = 2 * (token_count * top_count // experts)
    gate, up, down = gate_weight[0], up_weight[0], down_weight[0]

    def exchange(rows):
        moved = lax.all_to_all(rows.reshape(experts, chunk, width), "expert", split_axis=0, concat_axis=0, tiled=True)
        return moved.reshape(experts * chunk, width)

    choices, weights = routes.T, route_weights.T
    send = pack(tokens, cotangent, choices, weights, experts, chunk)
    inbox = exchange(send)
    back, inputs, out_grads, pair_grads, hidden = run_expert(inbox, gate, up, down, experts, 32)
    plan = plan_unpack(choices, weights, experts, chunk)
    returned = exchange(back)
    parts = weight_parts(inputs, out_grads, pair_grads, hidden)
    share = lax.psum_scatter(parts, "dp", scatter_dimension=0, tiled=True)
    return tuple(unpack(plan, returned, share))


def solution(mesh):
    rows = P(("dp", "expert"), None)
    expert = P("expert", None, None)
    return jax.shard_map(
        shards,
        mesh=mesh,
        in_specs=(rows, rows, rows, expert, expert, expert, rows),
        out_specs=(rows, rows, P("expert", "dp", None), P("expert", "dp", None), P("expert", None, "dp")),
        check_vma=False,
    )
```

```python
import jax
import jax.numpy as jnp
from jax import lax
from jax.experimental import pallas as pl
from jax.experimental.pallas import tpu as pltpu
from jax.sharding import PartitionSpec as P

INTERPRET = False
PACK_STEPS = 2
EXPERT_STEP = 32
F32 = jnp.float32
BF16 = jnp.bfloat16
NT = (((1,), (1,)), ((), ()))
HBM = pltpu.MemorySpace.HBM
VMEM = pltpu.MemorySpace.VMEM


def placed(array, space):
    return array if INTERPRET else pltpu.with_memory_space_constraint(array, space)


def made(shape, dtype, space):
    return jax.ShapeDtypeStruct(shape, dtype) if INTERPRET else space(shape, dtype)


def chunk_slot(row):
    slot = jnp.where(row < 12, row, jnp.where(row < 16, row - 4, row - 16))
    return slot.astype(F32), row >= 12


SIDE = 8


def expert_at(place):
    across, along = place // SIDE, place % SIDE
    return along * SIDE + (across + along) % SIDE


def route_tables(routes, weights, experts):
    top_count, token_count = routes.shape
    expert = expert_at(lax.broadcasted_iota(jnp.int32, (experts, token_count), 0))
    named = jnp.zeros((experts, token_count), F32)
    weight = jnp.zeros((experts, token_count), F32)
    for k in range(top_count):
        same = routes[k : k + 1, :] == expert
        named = jnp.where(same, 1.0, named)
        weight = jnp.where(same, weights[k : k + 1, :], weight)
    earlier = lax.broadcasted_iota(jnp.int32, (token_count, token_count), 0)
    later = lax.broadcasted_iota(jnp.int32, (token_count, token_count), 1)
    before = jnp.where(earlier < later, 1.0, 0.0).astype(BF16)
    rank = jnp.dot(named.astype(BF16), before, preferred_element_type=F32)
    return jnp.where(named > 0.0, rank, -1.0), weight


def pack_kernel(
    chunk, routes_hbm, weights_hbm, tokens_hbm, cot_hbm, send_ref, routes, weights, rows, rank_ref, weight_ref, sems
):
    token_count = routes.shape[1]
    total = rank_ref.shape[0]
    experts = send_ref.shape[0] // chunk
    step = pl.program_id(0)

    @pl.when(step == 0)
    def _():
        moves = [
            pltpu.make_async_copy(source, target, sems.at[i])
            for i, (source, target) in enumerate(
                [
                    (routes_hbm, routes),
                    (weights_hbm, weights),
                    (tokens_hbm, rows.at[pl.ds(0, token_count)]),
                    (cot_hbm, rows.at[pl.ds(token_count, token_count)]),
                ]
            )
        ]
        for move in moves:
            move.start()
        moves[0].wait()
        moves[1].wait()
        rank_ref[...], weight_ref[...] = route_tables(routes[...], weights[...], total)
        moves[2].wait()
        moves[3].wait()

    here = pl.ds(pl.multiple_of(step * experts, experts), experts)
    full = (experts, chunk, token_count)
    slot, backward = chunk_slot(lax.broadcasted_iota(jnp.int32, full, 1))
    hit = jnp.broadcast_to(rank_ref[here][:, None, :], full) == slot
    one = jnp.where(hit, 1.0, 0.0)
    forward_pick = jnp.where(backward, 0.0, one).reshape(experts * chunk, token_count).astype(BF16)
    backward_pick = jnp.where(backward, one, 0.0).reshape(experts * chunk, token_count).astype(BF16)
    chosen = jnp.where(hit, jnp.broadcast_to(weight_ref[here][:, None, :], full), 0.0)
    scale = jnp.where(backward, jnp.sum(chosen, axis=2, keepdims=True), 1.0).reshape(experts * chunk, token_count)
    pick = jnp.concatenate([forward_pick, backward_pick], axis=1)
    picked = jnp.dot(pick, rows[...], preferred_element_type=F32)
    for at in range(0, picked.shape[1], token_count):
        send_ref[:, at : at + token_count] = (picked[:, at : at + token_count] * scale).astype(BF16)


def pack(tokens, cotangent, routes, weights, experts, chunk):
    token_count, width = tokens.shape
    rows = experts * chunk
    steps = PACK_STEPS
    hbm = pl.BlockSpec(memory_space=pltpu.MemorySpace.HBM)
    return pl.pallas_call(
        lambda *refs: pack_kernel(chunk, *refs),
        grid=(steps,),
        in_specs=[hbm, hbm, hbm, hbm],
        out_specs=pl.BlockSpec((rows // steps, width), lambda i: (i, 0)),
        out_shape=jax.ShapeDtypeStruct((rows, width), BF16),
        scratch_shapes=[
            pltpu.VMEM(routes.shape, jnp.int32),
            pltpu.VMEM(weights.shape, F32),
            pltpu.VMEM((2 * token_count, width), BF16),
            pltpu.VMEM((experts, token_count), F32),
            pltpu.VMEM((experts, token_count), F32),
            pltpu.SemaphoreType.DMA((4,)),
        ],
        compiler_params=pltpu.CompilerParams(vmem_limit_bytes=28 * 1024 * 1024),
        cost_estimate=pl.CostEstimate(
            flops=4 * rows * token_count * width, bytes_accessed=2 * (rows + 2 * token_count) * width, transcendentals=0
        ),
        interpret=INTERPRET,
        name="pack",
    )(*(placed(array, HBM) for array in (routes, weights, tokens, cotangent)))


def plan_kernel(experts, chunk, routes_ref, weights_ref, plan_ref):
    token_count = routes_ref.shape[1]
    rank, weight = route_tables(routes_ref[...], weights_ref[...], 128)
    rank, weight = rank.T[:, :experts], weight.T[:, :experts]
    rows = experts * chunk
    owner = lax.broadcasted_iota(jnp.int32, (experts, rows), 0) * chunk
    place = lax.broadcasted_iota(jnp.int32, (experts, rows), 1) - owner
    spread = jnp.where((place >= 0) & (place < chunk), 1.0, 0.0).astype(BF16)

    def widen(values):
        return jnp.dot(values.astype(BF16), spread, preferred_element_type=F32)

    coarse = weight.astype(BF16).astype(F32)
    row = lax.rem(lax.broadcasted_iota(jnp.int32, (token_count, rows), 1), chunk)
    slot, backward = chunk_slot(row)
    hit = widen(rank) == slot
    ahead = jnp.where(backward, 0.0, jnp.where(hit, 1.0, 0.0))
    plan_ref[:token_count, :] = (widen(coarse) * ahead).astype(BF16)
    plan_ref[token_count : 2 * token_count, :] = (widen(weight - coarse) * ahead).astype(BF16)
    plan_ref[2 * token_count :, :] = jnp.where(backward & hit, 1.0, 0.0).astype(BF16)


def plan_unpack(routes, weights, experts, chunk):
    token_count = routes.shape[1]
    rows = experts * chunk
    return pl.pallas_call(
        lambda *refs: plan_kernel(experts, chunk, *refs),
        out_shape=jax.ShapeDtypeStruct((3 * token_count, rows), BF16),
        compiler_params=pltpu.CompilerParams(vmem_limit_bytes=28 * 1024 * 1024),
        cost_estimate=pl.CostEstimate(
            flops=6 * token_count * rows * experts, bytes_accessed=6 * token_count * rows, transcendentals=0
        ),
        interpret=INTERPRET,
        name="plan",
    )(routes, weights)


def unpack_kernel(plan_ref, back_ref, mixed_ref, grad_ref):
    token_count, width = mixed_ref.shape
    piece = 256
    for at in range(0, width, piece):
        cols = slice(at, at + piece)
        total = jnp.dot(plan_ref[...], back_ref[:, cols], preferred_element_type=F32)
        mixed_ref[:, cols] = (total[:token_count] + total[token_count : 2 * token_count]).astype(BF16)
        grad_ref[:, cols] = total[2 * token_count :].astype(BF16)


def unpack(plan, back):
    token_count = plan.shape[0] // 3
    rows, width = back.shape
    here = pl.BlockSpec(memory_space=VMEM)
    return pl.pallas_call(
        unpack_kernel,
        in_specs=[here, here],
        out_specs=[here, here],
        out_shape=[jax.ShapeDtypeStruct((token_count, width), BF16)] * 2,
        compiler_params=pltpu.CompilerParams(vmem_limit_bytes=28 * 1024 * 1024),
        cost_estimate=pl.CostEstimate(
            flops=6 * token_count * rows * width, bytes_accessed=2 * (rows + 5 * token_count) * width, transcendentals=0
        ),
        interpret=INTERPRET,
        name="unpack",
    )(placed(plan, VMEM), placed(back, VMEM))


def shard_dots(inputs_ref, grads_ref, pair_ref, hidden_ref):
    contract_rows = (((0,), (0,)), ((), ()))
    pair = lax.dot_general(inputs_ref[...], pair_ref[...], contract_rows, preferred_element_type=F32)
    down = lax.dot_general(grads_ref[...], hidden_ref[...], contract_rows, preferred_element_type=F32)
    return pair, down


def weight_kernel(first, place_ref, inputs_ref, grads_ref, pair_ref, hidden_ref, *refs):
    part_ref = refs[-1]
    both = pair_ref.shape[1]
    pair, down = shard_dots(inputs_ref, grads_ref, pair_ref, hidden_ref)
    if not first:
        pair = pair + refs[0][0, :, :both].astype(F32)
        down = down + refs[0][0, :, both:].astype(F32)
    part_ref[0, :, :both] = pair.astype(BF16)
    part_ref[0, :, both:] = down.astype(BF16)


def weight_half(place, inputs, grads, pair_grads, hidden, arrived, chips):
    slots, width = inputs.shape
    columns = pair_grads.shape[1] + hidden.shape[1]
    depth = width // (2 * chips)
    narrow = pl.BlockSpec((slots, depth), lambda i, at: (0, lax.rem(at[0] + i, chips) * 2 + at[1]))
    whole = lambda array: pl.BlockSpec(array.shape, lambda i, at: (0, 0))
    part = pl.BlockSpec((1, depth, columns), lambda i, at: (i, 0, 0))
    extra = [] if arrived is None else [arrived]
    return pl.pallas_call(
        lambda *refs: weight_kernel(arrived is None, *refs),
        grid_spec=pltpu.PrefetchScalarGridSpec(
            num_scalar_prefetch=1,
            grid=(chips,),
            in_specs=[narrow, narrow, whole(pair_grads), whole(hidden)] + [part for _ in extra],
            out_specs=part,
        ),
        out_shape=jax.ShapeDtypeStruct((chips, depth, columns), BF16),
        compiler_params=pltpu.CompilerParams(vmem_limit_bytes=28 * 1024 * 1024),
        cost_estimate=pl.CostEstimate(
            flops=slots * width * columns, bytes_accessed=2 * (slots + width) * columns, transcendentals=0
        ),
        interpret=INTERPRET,
        name="weight_half",
    )(place, inputs, grads, pair_grads, hidden, *extra)


def finish_kernel(*refs):
    gate_ref, up_ref, down_ref = refs[-3:]
    total = refs[0][0].astype(F32)
    for ref in refs[1:-3]:
        total = total + ref[0].astype(F32)
    ffn = gate_ref.shape[2]
    gate_ref[0] = total[:, :ffn]
    up_ref[0] = total[:, ffn : 2 * ffn]
    down_ref[0] = total[:, 2 * ffn :].T


def finish(shards_of):
    _, depth, columns = shards_of[0].shape
    ffn = columns // 3
    one = pl.BlockSpec((1, depth, columns), lambda: (0, 0, 0))
    return pl.pallas_call(
        finish_kernel,
        in_specs=[one for _ in shards_of],
        out_shape=[
            jax.ShapeDtypeStruct((1, depth, ffn), F32),
            jax.ShapeDtypeStruct((1, depth, ffn), F32),
            jax.ShapeDtypeStruct((1, ffn, depth), F32),
        ],
        compiler_params=pltpu.CompilerParams(vmem_limit_bytes=28 * 1024 * 1024),
        cost_estimate=pl.CostEstimate(
            flops=4 * depth * columns, bytes_accessed=12 * depth * columns, transcendentals=0
        ),
        interpret=INTERPRET,
        name="finish",
    )(*shards_of)


def roll_half(values):
    return pltpu.roll(values, 4, 1)


def split_slots(inbox_ref, tokens_ref, grads_ref):
    rows, width = inbox_ref.shape
    sources = rows // 24
    head = 8 * sources
    piece = 256
    for at in range(0, width, piece):
        cols = slice(at, at + piece)
        got = inbox_ref[:, cols].astype(F32).reshape(sources, 24, piece)
        both = got[:, 8:16].reshape(sources // 2, 2, 8, piece)
        first, second = both[:, 0], both[:, 1]
        low = lax.broadcasted_iota(jnp.int32, first.shape, 1) < 4
        tokens_ref[:head, cols] = got[:, :8].reshape(head, piece).astype(BF16)
        grads_ref[:head, cols] = got[:, 16:].reshape(head, piece).astype(BF16)
        tokens_ref[head:, cols] = jnp.where(low, first, roll_half(second)).reshape(-1, piece).astype(BF16)
        grads_ref[head:, cols] = jnp.where(low, roll_half(first), second).reshape(-1, piece).astype(BF16)


def sort_slots(inbox, sources, step):
    rows, width = inbox.shape
    slots = rows // 2
    part = lambda count: pl.BlockSpec((count, width), lambda i: (i, 0))
    return pl.pallas_call(
        split_slots,
        grid=(sources // step,),
        in_specs=[part(24 * step)],
        out_specs=[part(12 * step), part(12 * step)],
        out_shape=[jax.ShapeDtypeStruct((slots, width), BF16)] * 2,
        compiler_params=pltpu.CompilerParams(vmem_limit_bytes=28 * 1024 * 1024),
        cost_estimate=pl.CostEstimate(flops=4 * rows * width, bytes_accessed=4 * rows * width, transcendentals=0),
        interpret=INTERPRET,
        name="sort_slots",
    )(inbox)


def expert_kernel(
    sources, inbox_all, gate_ref, up_ref, down_ref, back_ref, pair_ref, hidden_ref, tokens_ref, grads_ref
):
    many = 24 * sources
    inbox_ref = inbox_all.at[pl.ds(pl.multiple_of(pl.program_id(0) * many, many), many)]
    width = inbox_ref.shape[1]
    ffn = gate_ref.shape[1]
    head = 8 * sources
    piece = 256
    split_slots(inbox_ref, tokens_ref, grads_ref)
    tokens, grads = tokens_ref[...], grads_ref[...]
    gate_pre = jnp.dot(tokens, gate_ref[...], preferred_element_type=F32)
    up_pre = jnp.dot(tokens, up_ref[...], preferred_element_type=F32)
    hidden_grad = lax.dot_general(grads, down_ref[...], NT, preferred_element_type=F32)
    sigmoid = jax.nn.sigmoid(gate_pre)
    silu = gate_pre * sigmoid
    hidden = (silu * up_pre).astype(BF16)
    up_grad_pre = (hidden_grad * silu).astype(BF16)
    gate_grad_pre = (hidden_grad * up_pre * sigmoid * (1.0 + gate_pre * (1.0 - sigmoid))).astype(BF16)
    hidden_ref[...] = hidden
    pair_ref[:, :ffn] = gate_grad_pre
    pair_ref[:, ffn:] = up_grad_pre
    for at in range(0, width, piece):
        cols = slice(at, at + piece)
        outputs = jnp.dot(hidden, down_ref[:, cols], preferred_element_type=F32)
        slot = lax.dot_general(gate_grad_pre, gate_ref[cols, :], NT, preferred_element_type=F32)
        slot = slot + lax.dot_general(up_grad_pre, up_ref[cols, :], NT, preferred_element_type=F32)
        out_tail = outputs[head:].reshape(sources // 2, 8, piece)
        slot_tail = slot[head:].reshape(sources // 2, 8, piece)
        low = lax.broadcasted_iota(jnp.int32, out_tail.shape, 1) < 4
        first = jnp.where(low, out_tail, roll_half(slot_tail))
        second = jnp.where(low, roll_half(out_tail), slot_tail)
        middle = jnp.concatenate([first[:, None], second[:, None]], axis=1).reshape(sources, 8, piece)
        sent = jnp.concatenate(
            [outputs[:head].reshape(sources, 8, piece), middle, slot[:head].reshape(sources, 8, piece)], axis=1
        )
        back_ref[:, cols] = sent.reshape(24 * sources, piece).astype(BF16)


def run_expert(inbox, gate, up, down, sources, step):
    rows, width = inbox.shape
    ffn = gate.shape[1]
    slots = rows // 2
    part = lambda count, columns: pl.BlockSpec((count, columns), lambda i: (i, 0))
    here = pl.BlockSpec(memory_space=VMEM)
    many, few = 24 * step, 12 * step
    return pl.pallas_call(
        lambda *refs: expert_kernel(step, *refs),
        grid=(sources // step,),
        in_specs=[here, here, here, here],
        out_specs=[part(many, width), part(few, 2 * ffn), part(few, ffn)],
        out_shape=[
            made((rows, width), BF16, HBM),
            made((slots, 2 * ffn), BF16, HBM),
            made((slots, ffn), BF16, HBM),
        ],
        scratch_shapes=[
            pltpu.VMEM((few, width), BF16),
            pltpu.VMEM((few, width), BF16),
        ],
        compiler_params=pltpu.CompilerParams(vmem_limit_bytes=28 * 1024 * 1024),
        cost_estimate=pl.CostEstimate(
            flops=12 * slots * width * ffn, bytes_accessed=14 * slots * width, transcendentals=slots * ffn
        ),
        interpret=INTERPRET,
        name="expert",
    )(*(placed(array, VMEM) for array in (inbox, gate, up, down)))


def shards(tokens, routes, route_weights, gate_weight, up_weight, down_weight, cotangent):
    token_count, width = tokens.shape
    top_count = routes.shape[1]
    experts = lax.axis_size("expert")
    chunk = 2 * (token_count * top_count // experts)
    gate, up, down = gate_weight[0], up_weight[0], down_weight[0]

    order = [[expert_at(place) for place in range(experts)]]

    def exchange(rows):
        moved = lax.all_to_all(rows.reshape(experts, chunk, width), "expert", split_axis=0, concat_axis=0, tiled=True, axis_index_groups=order)
        return moved.reshape(experts * chunk, width)

    choices, weights = routes.T, route_weights.T
    send = pack(tokens, cotangent, choices, weights, experts, chunk)
    inbox = exchange(send)
    back, pair_grads, hidden = run_expert(inbox, gate, up, down, experts, EXPERT_STEP)
    inputs, out_grads = sort_slots(inbox, experts, EXPERT_STEP)
    plan = plan_unpack(choices, weights, experts, chunk)
    returned = exchange(back)
    groups = lax.axis_size("dp")
    chips = groups // 2
    me = lax.axis_index("dp")
    chip, core = me // 2, me % 2
    work = (inputs, out_grads, pair_grads, hidden)
    other = weight_half(jnp.stack([chip, 1 - core]).astype(jnp.int32), *work, None, chips)
    arrived = lax.ppermute(other, "dp", [(d, d ^ 1) for d in range(groups)])
    mine = weight_half(jnp.stack([chip, core]).astype(jnp.int32), *work, arrived, chips)
    pieces = [mine[:1]]
    for step in range(1, chips):
        hop = [(d, (d + 2 * step) % groups) for d in range(groups)]
        pieces.append(lax.ppermute(mine[step : step + 1], "dp", hop))
    mixed_latent, latent_grad = unpack(plan, returned)
    return (mixed_latent, latent_grad, *finish(pieces))


def solution(mesh):
    rows = P(("dp", "expert"), None)
    expert = P("expert", None, None)
    return jax.shard_map(
        shards,
        mesh=mesh,
        in_specs=(rows, rows, rows, expert, expert, expert, rows),
        out_specs=(rows, rows, P("expert", "dp", None), P("expert", "dp", None), P("expert", None, "dp")),
        check_vma=False,
    )
```

```python
import jax
import jax.numpy as jnp
from jax import lax
from jax.experimental import pallas as pl
from jax.experimental.pallas import tpu as pltpu
from jax.sharding import PartitionSpec as P

INTERPRET = False
PACK_STEPS = 2
F32 = jnp.float32
BF16 = jnp.bfloat16
NT = (((1,), (1,)), ((), ()))
HBM = pltpu.MemorySpace.HBM
VMEM = pltpu.MemorySpace.VMEM


def placed(array, space):
    return array if INTERPRET else pltpu.with_memory_space_constraint(array, space)


def made(shape, dtype, space):
    return jax.ShapeDtypeStruct(shape, dtype) if INTERPRET else space(shape, dtype)


def chunk_slot(row):
    slot = jnp.where(row < 12, row, jnp.where(row < 16, row - 4, row - 16))
    return slot.astype(F32), row >= 12


SIDE = 8


def expert_at(place):
    across, along = place // SIDE, place % SIDE
    return along * SIDE + (along - across) % SIDE


def route_tables(routes, weights, experts):
    top_count, token_count = routes.shape
    expert = expert_at(lax.broadcasted_iota(jnp.int32, (experts, token_count), 0))
    named = jnp.zeros((experts, token_count), F32)
    weight = jnp.zeros((experts, token_count), F32)
    for k in range(top_count):
        same = routes[k : k + 1, :] == expert
        named = jnp.where(same, 1.0, named)
        weight = jnp.where(same, weights[k : k + 1, :], weight)
    earlier = lax.broadcasted_iota(jnp.int32, (token_count, token_count), 0)
    later = lax.broadcasted_iota(jnp.int32, (token_count, token_count), 1)
    before = jnp.where(earlier < later, 1.0, 0.0).astype(BF16)
    rank = jnp.dot(named.astype(BF16), before, preferred_element_type=F32)
    return jnp.where(named > 0.0, rank, -1.0), weight


def pack_kernel(
    chunk, routes_hbm, weights_hbm, tokens_hbm, cot_hbm, send_ref, routes, weights, rows, rank_ref, weight_ref, sems
):
    token_count = routes.shape[1]
    total = rank_ref.shape[0]
    experts = send_ref.shape[0] // chunk
    step = pl.program_id(0)

    @pl.when(step == 0)
    def _():
        moves = [
            pltpu.make_async_copy(source, target, sems.at[i])
            for i, (source, target) in enumerate(
                [
                    (routes_hbm, routes),
                    (weights_hbm, weights),
                    (tokens_hbm, rows.at[pl.ds(0, token_count)]),
                    (cot_hbm, rows.at[pl.ds(token_count, token_count)]),
                ]
            )
        ]
        for move in moves:
            move.start()
        moves[0].wait()
        moves[1].wait()
        rank_ref[...], weight_ref[...] = route_tables(routes[...], weights[...], total)
        moves[2].wait()
        moves[3].wait()

    here = pl.ds(pl.multiple_of(step * experts, experts), experts)
    full = (experts, chunk, token_count)
    slot, backward = chunk_slot(lax.broadcasted_iota(jnp.int32, full, 1))
    hit = jnp.broadcast_to(rank_ref[here][:, None, :], full) == slot
    one = jnp.where(hit, 1.0, 0.0)
    forward_pick = jnp.where(backward, 0.0, one).reshape(experts * chunk, token_count).astype(BF16)
    backward_pick = jnp.where(backward, one, 0.0).reshape(experts * chunk, token_count).astype(BF16)
    chosen = jnp.where(hit, jnp.broadcast_to(weight_ref[here][:, None, :], full), 0.0)
    scale = jnp.where(backward, jnp.sum(chosen, axis=2, keepdims=True), 1.0).reshape(experts * chunk, token_count)
    pick = jnp.concatenate([forward_pick, backward_pick], axis=1)
    picked = jnp.dot(pick, rows[...], preferred_element_type=F32)
    for at in range(0, picked.shape[1], token_count):
        send_ref[:, at : at + token_count] = (picked[:, at : at + token_count] * scale).astype(BF16)


def pack(tokens, cotangent, routes, weights, experts, chunk):
    token_count, width = tokens.shape
    rows = experts * chunk
    steps = PACK_STEPS
    hbm = pl.BlockSpec(memory_space=pltpu.MemorySpace.HBM)
    return pl.pallas_call(
        lambda *refs: pack_kernel(chunk, *refs),
        grid=(steps,),
        in_specs=[hbm, hbm, hbm, hbm],
        out_specs=pl.BlockSpec((rows // steps, width), lambda i: (i, 0)),
        out_shape=jax.ShapeDtypeStruct((rows, width), BF16),
        scratch_shapes=[
            pltpu.VMEM(routes.shape, jnp.int32),
            pltpu.VMEM(weights.shape, F32),
            pltpu.VMEM((2 * token_count, width), BF16),
            pltpu.VMEM((experts, token_count), F32),
            pltpu.VMEM((experts, token_count), F32),
            pltpu.SemaphoreType.DMA((4,)),
        ],
        compiler_params=pltpu.CompilerParams(vmem_limit_bytes=28 * 1024 * 1024),
        cost_estimate=pl.CostEstimate(
            flops=4 * rows * token_count * width, bytes_accessed=2 * (rows + 2 * token_count) * width, transcendentals=0
        ),
        interpret=INTERPRET,
        name="pack",
    )(*(placed(array, HBM) for array in (routes, weights, tokens, cotangent)))


def plan_kernel(experts, chunk, routes_ref, weights_ref, plan_ref):
    token_count = routes_ref.shape[1]
    rank, weight = route_tables(routes_ref[...], weights_ref[...], 128)
    rank, weight = rank.T[:, :experts], weight.T[:, :experts]
    rows = experts * chunk
    owner = lax.broadcasted_iota(jnp.int32, (experts, rows), 0) * chunk
    place = lax.broadcasted_iota(jnp.int32, (experts, rows), 1) - owner
    spread = jnp.where((place >= 0) & (place < chunk), 1.0, 0.0).astype(BF16)

    def widen(values):
        return jnp.dot(values.astype(BF16), spread, preferred_element_type=F32)

    coarse = weight.astype(BF16).astype(F32)
    row = lax.rem(lax.broadcasted_iota(jnp.int32, (token_count, rows), 1), chunk)
    slot, backward = chunk_slot(row)
    hit = widen(rank) == slot
    ahead = jnp.where(backward, 0.0, jnp.where(hit, 1.0, 0.0))
    plan_ref[:token_count, :] = (widen(coarse) * ahead).astype(BF16)
    plan_ref[token_count : 2 * token_count, :] = (widen(weight - coarse) * ahead).astype(BF16)
    plan_ref[2 * token_count :, :] = jnp.where(backward & hit, 1.0, 0.0).astype(BF16)


def plan_unpack(routes, weights, experts, chunk):
    token_count = routes.shape[1]
    rows = experts * chunk
    return pl.pallas_call(
        lambda *refs: plan_kernel(experts, chunk, *refs),
        out_shape=jax.ShapeDtypeStruct((3 * token_count, rows), BF16),
        compiler_params=pltpu.CompilerParams(vmem_limit_bytes=28 * 1024 * 1024),
        cost_estimate=pl.CostEstimate(
            flops=6 * token_count * rows * experts, bytes_accessed=6 * token_count * rows, transcendentals=0
        ),
        interpret=INTERPRET,
        name="plan",
    )(routes, weights)


def unpack_kernel(plan_ref, back_hbm, mixed_ref, grad_ref, back_ref, total_ref, sems):
    token_count = mixed_ref.shape[0]
    count = sems.shape[0]
    block = back_ref.shape[0] // count
    moves = []
    for i in range(count):
        rows = pl.ds(i * block, block)
        moves.append(pltpu.make_async_copy(back_hbm.at[rows], back_ref.at[rows], sems.at[i]))
        moves[-1].start()
    for i in range(count):
        rows = slice(i * block, (i + 1) * block)
        moves[i].wait()
        part = jnp.dot(plan_ref[:, rows], back_ref[rows], preferred_element_type=F32)
        if i == 0:
            total_ref[...] = part
        elif i < count - 1:
            total_ref[...] += part
        else:
            total = total_ref[...] + part
            mixed_ref[...] = (total[:token_count] + total[token_count : 2 * token_count]).astype(BF16)
            grad_ref[...] = total[2 * token_count :].astype(BF16)


def unpack(plan, back):
    token_count = plan.shape[0] // 3
    rows, width = back.shape
    here = pl.BlockSpec(memory_space=VMEM)
    return pl.pallas_call(
        unpack_kernel,
        in_specs=[here, pl.BlockSpec(memory_space=HBM)],
        out_specs=[here, here],
        out_shape=[jax.ShapeDtypeStruct((token_count, width), BF16)] * 2,
        scratch_shapes=[
            pltpu.VMEM((rows, width), BF16),
            pltpu.VMEM((plan.shape[0], width), F32),
            pltpu.SemaphoreType.DMA((4,)),
        ],
        compiler_params=pltpu.CompilerParams(vmem_limit_bytes=28 * 1024 * 1024),
        cost_estimate=pl.CostEstimate(
            flops=6 * token_count * rows * width, bytes_accessed=2 * (rows + 5 * token_count) * width, transcendentals=0
        ),
        interpret=INTERPRET,
        name="unpack",
    )(placed(plan, VMEM), placed(back, HBM))


def shard_dots(inputs_ref, grads_ref, pair_ref, hidden_ref):
    contract_rows = (((0,), (0,)), ((), ()))
    pair = lax.dot_general(inputs_ref[...], pair_ref[...], contract_rows, preferred_element_type=F32)
    down = lax.dot_general(grads_ref[...], hidden_ref[...], contract_rows, preferred_element_type=F32)
    return pair, down


def weight_kernel(first, place_ref, inputs_ref, grads_ref, pair_ref, hidden_ref, *refs):
    part_ref = refs[-1]
    both = pair_ref.shape[1]
    pair, down = shard_dots(inputs_ref, grads_ref, pair_ref, hidden_ref)
    if not first:
        pair = pair + refs[0][0, :, :both].astype(F32)
        down = down + refs[0][0, :, both:].astype(F32)
    part_ref[0, :, :both] = pair.astype(BF16)
    part_ref[0, :, both:] = down.astype(BF16)


def weight_half(place, inputs, grads, pair_grads, hidden, arrived, chips):
    slots, width = inputs.shape
    columns = pair_grads.shape[1] + hidden.shape[1]
    depth = width // (2 * chips)
    narrow = pl.BlockSpec((slots, depth), lambda i, at: (0, lax.rem(at[0] + i, chips) * 2 + at[1]))
    whole = lambda array: pl.BlockSpec(array.shape, lambda i, at: (0, 0))
    part = pl.BlockSpec((1, depth, columns), lambda i, at: (i, 0, 0))
    extra = [] if arrived is None else [arrived]
    return pl.pallas_call(
        lambda *refs: weight_kernel(arrived is None, *refs),
        grid_spec=pltpu.PrefetchScalarGridSpec(
            num_scalar_prefetch=1,
            grid=(chips,),
            in_specs=[narrow, narrow, whole(pair_grads), whole(hidden)] + [part for _ in extra],
            out_specs=part,
        ),
        out_shape=jax.ShapeDtypeStruct((chips, depth, columns), BF16),
        compiler_params=pltpu.CompilerParams(vmem_limit_bytes=28 * 1024 * 1024),
        cost_estimate=pl.CostEstimate(
            flops=slots * width * columns, bytes_accessed=2 * (slots + width) * columns, transcendentals=0
        ),
        interpret=INTERPRET,
        name="weight_half",
    )(place, inputs, grads, pair_grads, hidden, *extra)


def finish_kernel(*refs):
    gate_ref, up_ref, down_ref = refs[-3:]
    total = refs[0][0].astype(F32)
    for ref in refs[1:-3]:
        total = total + ref[0].astype(F32)
    ffn = gate_ref.shape[2]
    gate_ref[0] = total[:, :ffn]
    up_ref[0] = total[:, ffn : 2 * ffn]
    down_ref[0] = total[:, 2 * ffn :].T


def finish(shards_of):
    _, depth, columns = shards_of[0].shape
    ffn = columns // 3
    one = pl.BlockSpec((1, depth, columns), lambda: (0, 0, 0))
    return pl.pallas_call(
        finish_kernel,
        in_specs=[one for _ in shards_of],
        out_shape=[
            jax.ShapeDtypeStruct((1, depth, ffn), F32),
            jax.ShapeDtypeStruct((1, depth, ffn), F32),
            jax.ShapeDtypeStruct((1, ffn, depth), F32),
        ],
        compiler_params=pltpu.CompilerParams(vmem_limit_bytes=28 * 1024 * 1024),
        cost_estimate=pl.CostEstimate(
            flops=4 * depth * columns, bytes_accessed=12 * depth * columns, transcendentals=0
        ),
        interpret=INTERPRET,
        name="finish",
    )(*shards_of)


def roll_half(values):
    return pltpu.roll(values, 4, 1)


def split_slots(inbox_ref, tokens_ref, grads_ref):
    rows, width = inbox_ref.shape
    sources = rows // 24
    head = 8 * sources
    piece = 256
    for at in range(0, width, piece):
        cols = slice(at, at + piece)
        got = inbox_ref[:, cols].astype(F32).reshape(sources, 24, piece)
        both = got[:, 8:16].reshape(sources // 2, 2, 8, piece)
        first, second = both[:, 0], both[:, 1]
        low = lax.broadcasted_iota(jnp.int32, first.shape, 1) < 4
        tokens_ref[:head, cols] = got[:, :8].reshape(head, piece).astype(BF16)
        grads_ref[:head, cols] = got[:, 16:].reshape(head, piece).astype(BF16)
        tokens_ref[head:, cols] = jnp.where(low, first, roll_half(second)).reshape(-1, piece).astype(BF16)
        grads_ref[head:, cols] = jnp.where(low, roll_half(first), second).reshape(-1, piece).astype(BF16)


def sort_slots(inbox):
    rows, width = inbox.shape
    slots = rows // 2
    here = pl.BlockSpec(memory_space=VMEM)
    return pl.pallas_call(
        split_slots,
        in_specs=[here],
        out_specs=[here, here],
        out_shape=[jax.ShapeDtypeStruct((slots, width), BF16)] * 2,
        compiler_params=pltpu.CompilerParams(vmem_limit_bytes=28 * 1024 * 1024),
        cost_estimate=pl.CostEstimate(flops=4 * rows * width, bytes_accessed=4 * rows * width, transcendentals=0),
        interpret=INTERPRET,
        name="sort_slots",
    )(inbox)


def expert_kernel(
    inbox_ref, gate_ref, up_ref, down_ref, back_hbm, pair_hbm, hidden_hbm,
    tokens_ref, grads_ref, back_ref, pair_ref, hidden_ref, sems,
):
    rows, width = inbox_ref.shape
    ffn = gate_ref.shape[1]
    sources = rows // 24
    head = 8 * sources
    piece = 256
    moves = []

    def leave(source, target):
        moves.append(pltpu.make_async_copy(source, target, sems.at[len(moves)]))
        moves[-1].start()

    split_slots(inbox_ref, tokens_ref, grads_ref)
    for at in range(0, ffn, piece):
        cols = slice(at, at + piece)
        gate_pre = jnp.dot(tokens_ref[...], gate_ref[:, cols], preferred_element_type=F32)
        up_pre = jnp.dot(tokens_ref[...], up_ref[:, cols], preferred_element_type=F32)
        hidden_grad = lax.dot_general(grads_ref[...], down_ref[cols, :], NT, preferred_element_type=F32)
        sigmoid = jax.nn.sigmoid(gate_pre)
        silu = gate_pre * sigmoid
        hidden_ref[:, cols] = (silu * up_pre).astype(BF16)
        pair_ref[:, cols] = (hidden_grad * up_pre * sigmoid * (1.0 + gate_pre * (1.0 - sigmoid))).astype(BF16)
        pair_ref[:, ffn + at : ffn + at + piece] = (hidden_grad * silu).astype(BF16)
    leave(hidden_ref, hidden_hbm)
    leave(pair_ref, pair_hbm)
    for at in range(0, width, piece):
        cols = slice(at, at + piece)
        outputs = jnp.dot(hidden_ref[...], down_ref[:, cols], preferred_element_type=F32)
        slot = lax.dot_general(pair_ref[:, :ffn], gate_ref[cols, :], NT, preferred_element_type=F32)
        slot = slot + lax.dot_general(pair_ref[:, ffn:], up_ref[cols, :], NT, preferred_element_type=F32)
        out_tail = outputs[head:].reshape(sources // 2, 8, piece)
        slot_tail = slot[head:].reshape(sources // 2, 8, piece)
        low = lax.broadcasted_iota(jnp.int32, out_tail.shape, 1) < 4
        first = jnp.where(low, out_tail, roll_half(slot_tail))
        second = jnp.where(low, roll_half(out_tail), slot_tail)
        middle = jnp.concatenate([first[:, None], second[:, None]], axis=1).reshape(sources, 8, piece)
        sent = jnp.concatenate(
            [outputs[:head].reshape(sources, 8, piece), middle, slot[:head].reshape(sources, 8, piece)], axis=1
        )
        back_ref[:, cols] = sent.reshape(rows, piece).astype(BF16)
        leave(back_ref.at[:, cols], back_hbm.at[:, cols])
    for move in moves:
        move.wait()


def run_expert(inbox, gate, up, down):
    rows, width = inbox.shape
    ffn = gate.shape[1]
    slots = rows // 2
    here, there = pl.BlockSpec(memory_space=VMEM), pl.BlockSpec(memory_space=HBM)
    return pl.pallas_call(
        expert_kernel,
        in_specs=[here, here, here, here],
        out_specs=[there, there, there],
        out_shape=[
            made((rows, width), BF16, HBM),
            made((slots, 2 * ffn), BF16, HBM),
            made((slots, ffn), BF16, HBM),
        ],
        scratch_shapes=[
            pltpu.VMEM((slots, width), BF16),
            pltpu.VMEM((slots, width), BF16),
            pltpu.VMEM((rows, width), BF16),
            pltpu.VMEM((slots, 2 * ffn), BF16),
            pltpu.VMEM((slots, ffn), BF16),
            pltpu.SemaphoreType.DMA((2 + width // 256,)),
        ],
        compiler_params=pltpu.CompilerParams(vmem_limit_bytes=40 * 1024 * 1024),
        cost_estimate=pl.CostEstimate(
            flops=12 * slots * width * ffn, bytes_accessed=14 * slots * width, transcendentals=slots * ffn
        ),
        interpret=INTERPRET,
        name="expert",
    )(*(placed(array, VMEM) for array in (inbox, gate, up, down)))


def shards(tokens, routes, route_weights, gate_weight, up_weight, down_weight, cotangent):
    token_count, width = tokens.shape
    top_count = routes.shape[1]
    experts = lax.axis_size("expert")
    chunk = 2 * (token_count * top_count // experts)
    gate, up, down = gate_weight[0], up_weight[0], down_weight[0]

    order = [[expert_at(place) for place in range(experts)]]

    def exchange(rows):
        moved = lax.all_to_all(rows.reshape(experts, chunk, width), "expert", split_axis=0, concat_axis=0, tiled=True, axis_index_groups=order)
        return moved.reshape(experts * chunk, width)

    choices, weights = routes.T, route_weights.T
    send = pack(tokens, cotangent, choices, weights, experts, chunk)
    inbox = exchange(send)
    back, pair_grads, hidden = run_expert(inbox, gate, up, down)
    inputs, out_grads = sort_slots(inbox)
    plan = plan_unpack(choices, weights, experts, chunk)
    returned = exchange(back)
    groups = lax.axis_size("dp")
    chips = groups // 2
    me = lax.axis_index("dp")
    chip, core = me // 2, me % 2
    work = (inputs, out_grads, pair_grads, hidden)
    other = weight_half(jnp.stack([chip, 1 - core]).astype(jnp.int32), *work, None, chips)
    arrived = lax.ppermute(other, "dp", [(d, d ^ 1) for d in range(groups)])
    mine = weight_half(jnp.stack([chip, core]).astype(jnp.int32), *work, arrived, chips)
    pieces = [mine[:1]]
    for step in range(1, chips):
        hop = [(d, (d + 2 * step) % groups) for d in range(groups)]
        pieces.append(lax.ppermute(mine[step : step + 1], "dp", hop))
    mixed_latent, latent_grad = unpack(plan, returned)
    return (mixed_latent, latent_grad, *finish(pieces))


def solution(mesh):
    rows = P(("dp", "expert"), None)
    expert = P("expert", None, None)
    return jax.shard_map(
        shards,
        mesh=mesh,
        in_specs=(rows, rows, rows, expert, expert, expert, rows),
        out_specs=(rows, rows, P("expert", "dp", None), P("expert", "dp", None), P("expert", None, "dp")),
        check_vma=False,
    )
```

```python
import jax
import jax.numpy as jnp
from jax import lax
from jax.experimental import pallas as pl
from jax.experimental.pallas import tpu as pltpu
from jax.sharding import PartitionSpec as P

INTERPRET = False
PIECES = 4
F32 = jnp.float32
BF16 = jnp.bfloat16
NT = (((1,), (1,)), ((), ()))
HBM = pltpu.MemorySpace.HBM
VMEM = pltpu.MemorySpace.VMEM


def placed(array, space):
    return array if INTERPRET else pltpu.with_memory_space_constraint(array, space)


def made(shape, dtype, space):
    return jax.ShapeDtypeStruct(shape, dtype) if INTERPRET else space(shape, dtype)


def chunk_slot(row):
    slot = jnp.where(row < 12, row, jnp.where(row < 16, row - 4, row - 16))
    return slot.astype(F32), row >= 12


SIDE = 8


def expert_at(place):
    across, along = place // SIDE, place % SIDE
    return (across + 4 * along) % SIDE * SIDE + along


def route_tables(routes, weights, experts):
    top_count, token_count = routes.shape
    expert = expert_at(lax.broadcasted_iota(jnp.int32, (experts, token_count), 0))
    named = jnp.zeros((experts, token_count), F32)
    weight = jnp.zeros((experts, token_count), F32)
    for k in range(top_count):
        same = routes[k : k + 1, :] == expert
        named = jnp.where(same, 1.0, named)
        weight = jnp.where(same, weights[k : k + 1, :], weight)
    earlier = lax.broadcasted_iota(jnp.int32, (token_count, token_count), 0)
    later = lax.broadcasted_iota(jnp.int32, (token_count, token_count), 1)
    before = jnp.where(earlier < later, 1.0, 0.0).astype(BF16)
    rank = jnp.dot(named.astype(BF16), before, preferred_element_type=F32)
    return jnp.where(named > 0.0, rank, -1.0), weight


def pack_kernel(
    experts, chunk, routes_hbm, weights_hbm, tokens_hbm, cot_hbm, send_ref, routes, weights, rows, sems
):
    token_count = routes.shape[1]
    moves = [
        pltpu.make_async_copy(source, target, sems.at[i])
        for i, (source, target) in enumerate(
            [
                (routes_hbm, routes),
                (weights_hbm, weights),
                (tokens_hbm, rows.at[pl.ds(0, token_count)]),
                (cot_hbm, rows.at[pl.ds(token_count, token_count)]),
            ]
        )
    ]
    for move in moves:
        move.start()
    moves[0].wait()
    moves[1].wait()
    rank, weight = route_tables(routes[...], weights[...], experts)
    group = experts // 4
    full = (group, chunk, token_count)
    slot, backward = chunk_slot(lax.broadcasted_iota(jnp.int32, full, 1))
    for at in range(0, experts, group):
        hit = jnp.broadcast_to(rank[at : at + group][:, None, :], full) == slot
        one = jnp.where(hit, 1.0, 0.0)
        forward_pick = jnp.where(backward, 0.0, one).reshape(group * chunk, token_count).astype(BF16)
        backward_pick = jnp.where(backward, one, 0.0).reshape(group * chunk, token_count).astype(BF16)
        chosen = jnp.where(hit, jnp.broadcast_to(weight[at : at + group][:, None, :], full), 0.0)
        scale = jnp.where(backward, jnp.sum(chosen, axis=2, keepdims=True), 1.0).reshape(group * chunk, token_count)
        pick = jnp.concatenate([forward_pick, backward_pick], axis=1)
        if at == 0:
            moves[2].wait()
            moves[3].wait()
        picked = jnp.dot(pick, rows[...], preferred_element_type=F32)
        here = slice(at * chunk, (at + group) * chunk)
        for col in range(0, picked.shape[1], token_count):
            cols = slice(col, col + token_count)
            send_ref[here, cols] = (picked[:, cols] * scale).astype(BF16)


def pack(tokens, cotangent, routes, weights, experts, chunk):
    token_count, width = tokens.shape
    rows = experts * chunk
    hbm = pl.BlockSpec(memory_space=HBM)
    return pl.pallas_call(
        lambda *refs: pack_kernel(experts, chunk, *refs),
        in_specs=[hbm, hbm, hbm, hbm],
        out_specs=pl.BlockSpec(memory_space=VMEM),
        out_shape=made((rows, width), BF16, VMEM),
        scratch_shapes=[
            pltpu.VMEM(routes.shape, jnp.int32),
            pltpu.VMEM(weights.shape, F32),
            pltpu.VMEM((2 * token_count, width), BF16),
            pltpu.SemaphoreType.DMA((4,)),
        ],
        compiler_params=pltpu.CompilerParams(vmem_limit_bytes=14 * 1024 * 1024),
        cost_estimate=pl.CostEstimate(
            flops=4 * rows * token_count * width, bytes_accessed=2 * (rows + 2 * token_count) * width, transcendentals=0
        ),
        interpret=INTERPRET,
        name="pack",
    )(*(placed(array, HBM) for array in (routes, weights, tokens, cotangent)))


def plan_kernel(experts, chunk, routes_ref, weights_ref, plan_ref):
    token_count = routes_ref.shape[1]
    rank, weight = route_tables(routes_ref[...], weights_ref[...], 128)
    rank, weight = rank.T[:, :experts], weight.T[:, :experts]
    rows = experts * chunk
    owner = lax.broadcasted_iota(jnp.int32, (experts, rows), 0) * chunk
    place = lax.broadcasted_iota(jnp.int32, (experts, rows), 1) - owner
    spread = jnp.where((place >= 0) & (place < chunk), 1.0, 0.0).astype(BF16)

    def widen(values):
        return jnp.dot(values.astype(BF16), spread, preferred_element_type=F32)

    coarse = weight.astype(BF16).astype(F32)
    row = lax.rem(lax.broadcasted_iota(jnp.int32, (token_count, rows), 1), chunk)
    slot, backward = chunk_slot(row)
    hit = widen(rank) == slot
    ahead = jnp.where(backward, 0.0, jnp.where(hit, 1.0, 0.0))
    parts = [widen(coarse) * ahead, widen(weight - coarse) * ahead, jnp.where(backward & hit, 1.0, 0.0)]
    block = plan_ref.shape[1]
    for i, part in enumerate(parts):
        for at in range(0, rows, block):
            first = 3 * token_count * (at // block) + i * token_count
            plan_ref[first : first + token_count, :] = part[:, at : at + block].astype(BF16)


def plan_unpack(routes, weights, experts, chunk):
    token_count = routes.shape[1]
    rows = experts * chunk
    return pl.pallas_call(
        lambda *refs: plan_kernel(experts, chunk, *refs),
        out_shape=made((3 * token_count * PIECES, rows // PIECES), BF16, HBM),
        compiler_params=pltpu.CompilerParams(vmem_limit_bytes=14 * 1024 * 1024),
        cost_estimate=pl.CostEstimate(
            flops=6 * token_count * rows * experts, bytes_accessed=6 * token_count * rows, transcendentals=0
        ),
        interpret=INTERPRET,
        name="plan",
    )(routes, weights)


def unpack_kernel(plan_hbm, back_ref, mixed_ref, grad_ref, plan_ref, total_ref, sems):
    token_count = mixed_ref.shape[0]
    block = back_ref.shape[0] // PIECES
    deep = 3 * token_count
    moves = []
    for i in range(PIECES):
        rows = pl.ds(i * deep, deep)
        moves.append(pltpu.make_async_copy(plan_hbm.at[rows], plan_ref.at[rows], sems.at[i]))
        moves[-1].start()
    for i in range(PIECES):
        moves[i].wait()
        chosen = plan_ref[i * deep : (i + 1) * deep]
        part = jnp.dot(chosen, back_ref[i * block : (i + 1) * block], preferred_element_type=F32)
        if i == 0:
            total_ref[...] = part
        elif i < PIECES - 1:
            total_ref[...] += part
        else:
            total = total_ref[...] + part
            mixed_ref[...] = (total[:token_count] + total[token_count : 2 * token_count]).astype(BF16)
            grad_ref[...] = total[2 * token_count :].astype(BF16)


def unpack(plan, back):
    token_count = plan.shape[0] // (3 * PIECES)
    rows, width = back.shape
    here = pl.BlockSpec(memory_space=VMEM)
    return pl.pallas_call(
        unpack_kernel,
        in_specs=[pl.BlockSpec(memory_space=HBM), here],
        out_specs=[here, here],
        out_shape=[jax.ShapeDtypeStruct((token_count, width), BF16)] * 2,
        scratch_shapes=[
            pltpu.VMEM(plan.shape, BF16),
            pltpu.VMEM((3 * token_count, width), F32),
            pltpu.SemaphoreType.DMA((PIECES,)),
        ],
        compiler_params=pltpu.CompilerParams(vmem_limit_bytes=14 * 1024 * 1024),
        cost_estimate=pl.CostEstimate(
            flops=6 * token_count * rows * width, bytes_accessed=2 * (rows + 5 * token_count) * width, transcendentals=0
        ),
        interpret=INTERPRET,
        name="unpack",
    )(placed(plan, HBM), back)


def shard_dots(inputs_ref, grads_ref, pair_ref, hidden_ref):
    contract_rows = (((0,), (0,)), ((), ()))
    pair = lax.dot_general(inputs_ref[...], pair_ref[...], contract_rows, preferred_element_type=F32)
    down = lax.dot_general(grads_ref[...], hidden_ref[...], contract_rows, preferred_element_type=F32)
    return pair, down


def weight_kernel(first, place_ref, inputs_ref, grads_ref, pair_ref, hidden_ref, *refs):
    part_ref = refs[-1]
    both = pair_ref.shape[1]
    pair, down = shard_dots(inputs_ref, grads_ref, pair_ref, hidden_ref)
    if not first:
        pair = pair + refs[0][0, :, :both].astype(F32)
        down = down + refs[0][0, :, both:].astype(F32)
    part_ref[0, :, :both] = pair.astype(BF16)
    part_ref[0, :, both:] = down.astype(BF16)


def weight_half(place, inputs, grads, pair_grads, hidden, arrived, chips):
    slots, width = inputs.shape
    columns = pair_grads.shape[1] + hidden.shape[1]
    depth = width // (2 * chips)
    narrow = pl.BlockSpec((slots, depth), lambda i, at: (0, lax.rem(at[0] + i, chips) * 2 + at[1]))
    whole = lambda array: pl.BlockSpec(array.shape, lambda i, at: (0, 0))
    part = pl.BlockSpec((1, depth, columns), lambda i, at: (i, 0, 0))
    extra = [] if arrived is None else [arrived]
    return pl.pallas_call(
        lambda *refs: weight_kernel(arrived is None, *refs),
        grid_spec=pltpu.PrefetchScalarGridSpec(
            num_scalar_prefetch=1,
            grid=(chips,),
            in_specs=[narrow, narrow, whole(pair_grads), whole(hidden)] + [part for _ in extra],
            out_specs=part,
        ),
        out_shape=jax.ShapeDtypeStruct((chips, depth, columns), BF16),
        compiler_params=pltpu.CompilerParams(vmem_limit_bytes=14 * 1024 * 1024),
        cost_estimate=pl.CostEstimate(
            flops=slots * width * columns, bytes_accessed=2 * (slots + width) * columns, transcendentals=0
        ),
        interpret=INTERPRET,
        name="weight_half",
    )(place, inputs, grads, pair_grads, hidden, *extra)


def finish_kernel(*refs):
    gate_ref, up_ref, down_ref = refs[-3:]
    total = refs[0][0].astype(F32)
    for ref in refs[1:-3]:
        total = total + ref[0].astype(F32)
    ffn = gate_ref.shape[2]
    gate_ref[0] = total[:, :ffn]
    up_ref[0] = total[:, ffn : 2 * ffn]
    down_ref[0] = total[:, 2 * ffn :].T


def finish(shards_of):
    _, depth, columns = shards_of[0].shape
    ffn = columns // 3
    one = pl.BlockSpec((1, depth, columns), lambda: (0, 0, 0))
    return pl.pallas_call(
        finish_kernel,
        in_specs=[one for _ in shards_of],
        out_shape=[
            jax.ShapeDtypeStruct((1, depth, ffn), F32),
            jax.ShapeDtypeStruct((1, depth, ffn), F32),
            jax.ShapeDtypeStruct((1, ffn, depth), F32),
        ],
        compiler_params=pltpu.CompilerParams(vmem_limit_bytes=14 * 1024 * 1024),
        cost_estimate=pl.CostEstimate(
            flops=4 * depth * columns, bytes_accessed=12 * depth * columns, transcendentals=0
        ),
        interpret=INTERPRET,
        name="finish",
    )(*shards_of)


def roll_half(values):
    return pltpu.roll(values, 4, 1)


def split_slots(inbox_ref, tokens_ref, grads_ref):
    rows, width = inbox_ref.shape
    sources = rows // 24
    head = 8 * sources
    piece = 256
    for at in range(0, width, piece):
        cols = slice(at, at + piece)
        got = inbox_ref[:, cols].astype(F32).reshape(sources, 24, piece)
        both = got[:, 8:16].reshape(sources // 2, 2, 8, piece)
        first, second = both[:, 0], both[:, 1]
        low = lax.broadcasted_iota(jnp.int32, first.shape, 1) < 4
        tokens_ref[:head, cols] = got[:, :8].reshape(head, piece).astype(BF16)
        grads_ref[:head, cols] = got[:, 16:].reshape(head, piece).astype(BF16)
        tokens_ref[head:, cols] = jnp.where(low, first, roll_half(second)).reshape(-1, piece).astype(BF16)
        grads_ref[head:, cols] = jnp.where(low, roll_half(first), second).reshape(-1, piece).astype(BF16)


def hidden_parts(gate_ref, up_ref, down_ref, tokens_ref, grads_ref, pair_ref, hidden_ref):
    ffn = gate_ref.shape[1]
    piece = 256
    for at in range(0, ffn, piece):
        cols = slice(at, at + piece)
        gate_pre = jnp.dot(tokens_ref[...], gate_ref[:, cols], preferred_element_type=F32)
        up_pre = jnp.dot(tokens_ref[...], up_ref[:, cols], preferred_element_type=F32)
        hidden_grad = lax.dot_general(grads_ref[...], down_ref[cols, :], NT, preferred_element_type=F32)
        sigmoid = jax.nn.sigmoid(gate_pre)
        silu = gate_pre * sigmoid
        hidden_ref[:, cols] = (silu * up_pre).astype(BF16)
        pair_ref[:, cols] = (hidden_grad * up_pre * sigmoid * (1.0 + gate_pre * (1.0 - sigmoid))).astype(BF16)
        pair_ref[:, ffn + at : ffn + at + piece] = (hidden_grad * silu).astype(BF16)


def again_kernel(inbox_ref, gate_ref, up_ref, down_ref, tokens_ref, grads_ref, pair_ref, hidden_ref):
    split_slots(inbox_ref, tokens_ref, grads_ref)
    hidden_parts(gate_ref, up_ref, down_ref, tokens_ref, grads_ref, pair_ref, hidden_ref)


def parts_again(inbox, gate, up, down):
    rows, width = inbox.shape
    ffn = gate.shape[1]
    slots = rows // 2
    here = pl.BlockSpec(memory_space=VMEM)
    return pl.pallas_call(
        again_kernel,
        in_specs=[here, here, here, here],
        out_specs=[here, here, here, here],
        out_shape=[
            jax.ShapeDtypeStruct((slots, width), BF16),
            jax.ShapeDtypeStruct((slots, width), BF16),
            jax.ShapeDtypeStruct((slots, 2 * ffn), BF16),
            jax.ShapeDtypeStruct((slots, ffn), BF16),
        ],
        compiler_params=pltpu.CompilerParams(vmem_limit_bytes=14 * 1024 * 1024),
        cost_estimate=pl.CostEstimate(
            flops=6 * slots * width * ffn, bytes_accessed=12 * slots * width, transcendentals=slots * ffn
        ),
        interpret=INTERPRET,
        name="parts_again",
    )(inbox, gate, up, down)


def expert_kernel(
    inbox_ref, gate_ref, up_ref, down_ref, back_hbm,
    tokens_ref, grads_ref, back_ref, pair_ref, hidden_ref, sems,
):
    rows, width = inbox_ref.shape
    ffn = gate_ref.shape[1]
    sources = rows // 24
    head = 8 * sources
    piece = 256
    moves = []

    def leave(source, target):
        moves.append(pltpu.make_async_copy(source, target, sems.at[len(moves)]))
        moves[-1].start()

    split_slots(inbox_ref, tokens_ref, grads_ref)
    hidden_parts(gate_ref, up_ref, down_ref, tokens_ref, grads_ref, pair_ref, hidden_ref)
    half = sources // 2
    for start in range(0, sources, half):
        mine = [
            slice(8 * start, 8 * (start + half)),
            slice(head + 4 * start, head + 4 * (start + half)),
        ]

        def some(ref, cols):
            return jnp.concatenate([ref[rows, cols] for rows in mine], axis=0)

        hidden = some(hidden_ref, slice(None))
        gate_grad_pre, up_grad_pre = some(pair_ref, slice(0, ffn)), some(pair_ref, slice(ffn, 2 * ffn))
        here = slice(24 * start, 24 * (start + half))
        for at in range(0, width, piece):
            cols = slice(at, at + piece)
            outputs = jnp.dot(hidden, down_ref[:, cols], preferred_element_type=F32)
            slot = lax.dot_general(gate_grad_pre, gate_ref[cols, :], NT, preferred_element_type=F32)
            slot = slot + lax.dot_general(up_grad_pre, up_ref[cols, :], NT, preferred_element_type=F32)
            out_tail = outputs[8 * half :].reshape(half // 2, 8, piece)
            slot_tail = slot[8 * half :].reshape(half // 2, 8, piece)
            low = lax.broadcasted_iota(jnp.int32, out_tail.shape, 1) < 4
            first = jnp.where(low, out_tail, roll_half(slot_tail))
            second = jnp.where(low, roll_half(out_tail), slot_tail)
            middle = jnp.concatenate([first[:, None], second[:, None]], axis=1).reshape(half, 8, piece)
            sent = jnp.concatenate(
                [outputs[: 8 * half].reshape(half, 8, piece), middle, slot[: 8 * half].reshape(half, 8, piece)], axis=1
            )
            back_ref[here, cols] = sent.reshape(24 * half, piece).astype(BF16)
        leave(back_ref.at[here], back_hbm.at[here])
    for move in moves:
        move.wait()


def run_expert(inbox, gate, up, down):
    rows, width = inbox.shape
    ffn = gate.shape[1]
    slots = rows // 2
    here, there = pl.BlockSpec(memory_space=VMEM), pl.BlockSpec(memory_space=HBM)
    return pl.pallas_call(
        expert_kernel,
        in_specs=[here, here, here, here],
        out_specs=there,
        out_shape=made((rows, width), BF16, HBM),
        scratch_shapes=[
            pltpu.VMEM((slots, width), BF16),
            pltpu.VMEM((slots, width), BF16),
            pltpu.VMEM((rows, width), BF16),
            pltpu.VMEM((slots, 2 * ffn), BF16),
            pltpu.VMEM((slots, ffn), BF16),
            pltpu.SemaphoreType.DMA((2,)),
        ],
        compiler_params=pltpu.CompilerParams(vmem_limit_bytes=40 * 1024 * 1024),
        cost_estimate=pl.CostEstimate(
            flops=12 * slots * width * ffn, bytes_accessed=14 * slots * width, transcendentals=slots * ffn
        ),
        interpret=INTERPRET,
        name="expert",
    )(*(placed(array, VMEM) for array in (inbox, gate, up, down)))


def shards(tokens, routes, route_weights, gate_weight, up_weight, down_weight, cotangent):
    token_count, width = tokens.shape
    top_count = routes.shape[1]
    experts = lax.axis_size("expert")
    chunk = 2 * (token_count * top_count // experts)
    gate, up, down = gate_weight[0], up_weight[0], down_weight[0]

    order = [[expert_at(place) for place in range(experts)]]

    def exchange(rows):
        moved = lax.all_to_all(rows.reshape(experts, chunk, width), "expert", split_axis=0, concat_axis=0, tiled=True, axis_index_groups=order)
        return moved.reshape(experts * chunk, width)

    choices, weights = routes.T, route_weights.T
    send = pack(tokens, cotangent, choices, weights, experts, chunk)
    inbox = exchange(send)
    back = run_expert(inbox, gate, up, down)
    inputs, out_grads, pair_grads, hidden = parts_again(inbox, gate, up, down)
    plan = plan_unpack(choices, weights, experts, chunk)
    returned = exchange(back)
    groups = lax.axis_size("dp")
    chips = groups // 2
    me = lax.axis_index("dp")
    chip, core = me // 2, me % 2
    work = (inputs, out_grads, pair_grads, hidden)
    other = weight_half(jnp.stack([chip, 1 - core]).astype(jnp.int32), *work, None, chips)
    arrived = lax.ppermute(other, "dp", [(d, d ^ 1) for d in range(groups)])
    mine = weight_half(jnp.stack([chip, core]).astype(jnp.int32), *work, arrived, chips)
    pieces = [mine[:1]]
    for step in range(1, chips):
        hop = [(d, (d + 2 * step) % groups) for d in range(groups)]
        pieces.append(lax.ppermute(mine[step : step + 1], "dp", hop))
    mixed_latent, latent_grad = unpack(plan, returned)
    return (mixed_latent, latent_grad, *finish(pieces))


def solution(mesh):
    rows = P(("dp", "expert"), None)
    expert = P("expert", None, None)
    return jax.shard_map(
        shards,
        mesh=mesh,
        in_specs=(rows, rows, rows, expert, expert, expert, rows),
        out_specs=(rows, rows, P("expert", "dp", None), P("expert", "dp", None), P("expert", None, "dp")),
        check_vma=False,
    )
```
